256 devices in a mesh: blk: 32 (over z, y), rep: 8 (over x, core).
Axes of the slice: x: 4, y: 4, z: 8, core: 2. Of those that a mesh axis runs over, the one named last changes fastest.
Arguments:
- three_centre: bfloat16 [32, 7, 116, 29696], P('blk', None, None, 'rep'), may hold values from -0.21875 to 0.21875
- coeffs: bfloat16 [3712, 160], P('blk'), may hold values from -6 to 6
- neighbours: int32 [32, 7], P('blk'), may hold values from 0 to 31, as said below
- counts: int32 [32], P('blk'), may hold values from 1 to 7, as said below
Outputs:
- exchange_orbitals: float32 [3712, 160], P('blk', 'rep')
The draws below stay inside these ranges and needn't reach their ends.
Inputs may be any that keep to these rules, and one draw needn't show every extreme that they name: `neighbours`: each row holds distinct molecules, the row's own molecule in slot 0. `counts`: in every draw some molecule uses all 7 slots.
All inputs are finite; a program needn't handle non-finite values.
Results may differ from the reference program's by a relative error of at most 0.0013.
Values may be sent and summed in bfloat16 or wider, within the bound.
A program may use at most 64 MiB of HBM per device.

```python
import math
import jax
import jax.numpy as jnp
from jax import lax

BS = 116
NLIST = 7
NMOL = 32
N = 3712
OCC = 160
NAT = 256


def draw_neighbours(key, part):
    key = jax.random.fold_in(key, 11)
    row_keys = jax.random.split(key, NMOL)
    orders = jax.vmap(lambda each: jax.random.permutation(each, NMOL - 1))(row_keys)[:, :NLIST - 1]
    rows = jnp.arange(NMOL)[:, None]
    return jnp.concatenate([rows, (rows + 1 + orders) % NMOL], axis=1).astype(jnp.int32)


def draw_counts(key, part):
    key = jax.random.fold_in(key, 23)
    first, second = jax.random.split(key)
    drawn = jax.random.randint(first, (NMOL,), 1, NLIST + 1)
    place = jax.random.randint(second, (), 0, NMOL)
    return jnp.where(jnp.arange(NMOL) == place, NLIST, drawn).astype(jnp.int32)


def levels(rng, dims, pieces, least, largest):
    def one(axis_at, shards_of):
        draws = jax.random.uniform(jax.random.fold_in(jax.random.fold_in(rng, 6), axis_at), (shards_of,), jnp.float32, least / len(pieces), largest / len(pieces))
        return jnp.repeat(jnp.exp(draws), dims[axis_at] // shards_of).reshape((-1,) + (1,) * (len(dims) - axis_at - 1))

    gain = one(*pieces[0])
    for cut in pieces[1:]:
        gain = gain * one(*cut)
    return gain


def bell_draw(rng, shape, deviation, reach, cuts=(), kind=jnp.bfloat16):
    gain = levels(rng, shape, cuts, -0.22, 0.18) if cuts else 1.0
    values = jax.random.normal(rng, shape, jnp.float32) * deviation * gain
    return jnp.minimum(jnp.maximum(values, -reach), reach).astype(kind)


def setup_inputs(seed: int = 0) -> dict:
    arg_keys = jax.random.split(jax.random.key(seed), 5)
    three_centre = bell_draw(arg_keys[0], (NMOL, NLIST, BS, NAT * BS), (NLIST * BS) ** -0.5, 0.21875, ((0, 32), (3, 8)))
    coeffs = bell_draw(arg_keys[1], (N, OCC), 1.0, 6.0, ((0, 32),))
    neighbours = draw_neighbours(jax.random.fold_in(arg_keys[4], 71), 0)
    counts = draw_counts(jax.random.fold_in(arg_keys[4], 71), 0)
    return dict(three_centre=three_centre, coeffs=coeffs, neighbours=neighbours, counts=counts)


def reference(three_centre, coeffs, neighbours, counts):
    nmol, nlist, bs, width = three_centre.shape
    occ = coeffs.shape[1]
    total = nmol * bs
    naux = width // bs
    blocks = coeffs.reshape(nmol, bs, occ)
    used = (jnp.arange(nlist)[None, :] < counts[:, None]).astype(jnp.bfloat16)

    def one_molecule(index):
        picked = blocks[neighbours[index]] * used[index][:, None, None]
        left = three_centre[index].reshape(nlist * bs, width)
        product = lax.dot_general(left, picked.reshape(nlist * bs, occ), (((0,), (0,)), ((), ())), preferred_element_type=jnp.float32)
        return product.astype(jnp.bfloat16).reshape(naux, bs, occ)
    halves = lax.map(one_molecule, jnp.arange(nmol))
    halves = jnp.transpose(halves, (1, 0, 2, 3)).reshape(naux, total, occ)
    mscale = 1.0 / math.sqrt(total)

    def accumulate(carry, rows):
        pairs = jnp.dot(rows.T, coeffs, preferred_element_type=jnp.float32)
        pairs = (pairs * mscale).astype(jnp.bfloat16)
        return (carry + jnp.dot(rows, pairs, preferred_element_type=jnp.float32), None)
    result, unused = lax.scan(accumulate, jnp.zeros((total, occ), jnp.float32), halves)
    return result * (1.0 / math.sqrt(naux * occ))
```

```python
import functools
import math

import jax
import jax.numpy as jnp
from jax import lax
from jax.experimental import pallas as pl
from jax.experimental.pallas import tpu as pltpu
from jax.sharding import PartitionSpec as P

MESH = pl.DeviceIdType.MESH
NZ, NY, NX, NC = 8, 4, 4, 2
CHUNKS = ((0, 64), (64, 96))
BF16, F32 = jnp.bfloat16, jnp.float32


def kernel(
    t_ref, c_ref, nbr_ref, cnt_ref, o_ref,
    tv, tp, own, ct, ctp, pk, h, hs, hr, prf, prb, rsb, pf, oacc, frecv, fsum, f2,
    t_sem, s1s, s1r, s2s, s2r, cs, cr, a2s, a2r, rss, rsr, ags, agr, f1s, f1r, f2s, f2r,
):
    occ, bs = c_ref.shape
    nlist = t_ref.shape[1]
    width = t_ref.shape[3]
    naux = width // bs
    total = bs * NZ * NY
    mscale = 1.0 / math.sqrt(total)
    oscale = 1.0 / math.sqrt(naux * NX * NC * occ)
    blk, rep = lax.axis_index("blk"), lax.axis_index("rep")
    z, y, x, c = blk // NY, blk % NY, rep // NC, rep % NC
    zh, zl = z // 2, z % 2
    m_me = y * 2 + zl

    def dev(z_, y_, x_, c_):
        return (z_ * NY + y_, x_ * NC + c_)

    loads = [pltpu.make_async_copy(t_ref.at[0, l], tv.at[l], t_sem.at[l]) for l in range(nlist)]
    for load in loads:
        load.start()

    rel = [(dx, dy, dl) for dx in range(NX) for dy in range(NY) for dl in range(2)][1:]
    cls = x * NC + c
    self_here = cls == 0

    def s1_shift(dy):
        return lax.rem(cls + 2 * dy, NZ)

    def rel_dev(dx, dy, dl):
        return dev(zh * 2 + (zl + dl) % 2, (y + dy) % NY, (x + dx) % NX, c)

    sibling = dev(z, y, x, 1 - c)
    barrier = pltpu.get_barrier_semaphore()

    def hello(device):
        pl.semaphore_signal(barrier, inc=1, device_id=device, device_id_type=MESH)

    for r in rel:
        hello(rel_dev(*r))
    hello(sibling)
    for d in range(1, NZ // 2):
        hello(dev((z + 2 * d) % NZ, y, x, c))
    for dy in range(NY):
        source = dev((z + NZ - s1_shift(dy)) % NZ, (y + NY - dy) % NY, x, c)
        if dy == 0:
            pl.when(jnp.logical_not(self_here))(functools.partial(hello, source))
        else:
            hello(source)

    own[...] = jnp.concatenate([c_ref[...], jnp.zeros((occ, 128 - bs), BF16)], axis=1)

    count = len(rel) + 1 + (NZ // 2 - 1) + NY
    pl.semaphore_wait(barrier, jnp.where(self_here, count - 1, count))

    def s1_copy(ch, dy):
        r0, w = CHUNKS[ch]
        rows = pl.ds(r0, w)
        return pltpu.make_async_remote_copy(
            src_ref=own.at[rows, :], dst_ref=ct[ch].at[c, x, dy],
            send_sem=s1s.at[ch, dy], recv_sem=s1r.at[ch, dy],
            device_id=dev((z + s1_shift(dy)) % NZ, (y + dy) % NY, x, c), device_id_type=MESH,
        )

    def s1_local(ch):
        r0, w = CHUNKS[ch]
        rows = pl.ds(r0, w)
        return pltpu.make_async_copy(own.at[rows, :], ct[ch].at[c, x, 0], s1r.at[ch, 0])

    for ch in range(len(CHUNKS)):
        for dy in range(1, NY):
            s1_copy(ch, dy).start()
        pl.when(jnp.logical_not(self_here))(lambda ch=ch: s1_copy(ch, 0).start())
        pl.when(self_here)(lambda ch=ch: s1_local(ch).start())

    def s1_wait(ch):
        for dy in range(1, NY):
            s1_copy(ch, dy).wait_recv()
        pl.when(jnp.logical_not(self_here))(lambda: s1_copy(ch, 0).wait_recv())
        pl.when(self_here)(lambda: s1_local(ch).wait())

    def s2_copy(ch, d, x_src):
        part = ct[ch].at[c, x_src]
        return pltpu.make_async_remote_copy(
            src_ref=part, dst_ref=part, send_sem=s2s.at[ch, d - 1], recv_sem=s2r.at[ch, d - 1],
            device_id=dev(z, y, (x + d) % NX, c), device_id_type=MESH,
        )

    def core_copy(ch, c_src):
        part = ct[ch].at[c_src]
        return pltpu.make_async_remote_copy(
            src_ref=part, dst_ref=part, send_sem=cs.at[ch], recv_sem=cr.at[ch],
            device_id=sibling, device_id_type=MESH,
        )

    for l in range(nlist):
        loads[l].wait()
        top = bs // 16 * 16
        tp[l * 128 : l * 128 + top, :] = tv[l, 0:top, :]
        tail = tv[l, top:bs, :]
        tp[l * 128 + top : (l + 1) * 128, :] = jnp.concatenate(
            [tail, jnp.zeros((128 - bs, width), BF16)], axis=0
        )

    for ch in range(len(CHUNKS)):
        s1_wait(ch)
        for d in range(1, NX):
            s2_copy(ch, d, x).start()

    def place(b):
        zb, yb = b // NY, b % NY
        dy = (y + NY - yb) % NY
        s = (z + 2 * NZ - zb - 2 * dy) % NZ
        return s % NC, s // NC, dy

    def a2a_copy(ch, dy, dl, recv):
        w = CHUNKS[ch][1]
        y_, l_ = (y + dy) % NY, (zl + dl) % 2
        if recv:
            y_ = (y + NY - dy) % NY
            lanes = pl.ds(pl.multiple_of((y_ * 2 + l_) * 128, 128), 128)
        else:
            lanes = pl.ds(pl.multiple_of(m_me * 128, 128), 128)
        k = dy * 2 + dl
        return pltpu.make_async_remote_copy(
            src_ref=hs[ch].at[y_ * 2 + l_], dst_ref=hr[ch].at[:, lanes],
            send_sem=a2s.at[ch, k], recv_sem=a2r.at[ch, k],
            device_id=rel_dev(0, dy, dl), device_id_type=MESH,
        )

    def a2a_local(ch):
        lanes = pl.ds(pl.multiple_of(m_me * 128, 128), 128)
        return pltpu.make_async_copy(hs[ch].at[m_me], hr[ch].at[:, lanes], a2r.at[ch, 0])

    near = [(dy, dl) for dy in range(NY) for dl in range(2)][1:]

    for ch, (r0, w) in enumerate(CHUNKS):
        for d in range(1, NX):
            s2_copy(ch, d, (x + NX - d) % NX).wait_recv()
        core_copy(ch, c).start()
        core_copy(ch, 1 - c).wait_recv()
        for l in range(nlist):
            if l == 0:
                block = own[r0 : r0 + w, :]
            else:
                c_, x_, dy_ = place(nbr_ref[0, l])
                block = ct[ch][c_, x_, dy_]
            block = jnp.where(l < cnt_ref[0], block, jnp.zeros_like(block))
            pk[ch][:, l * 128 : (l + 1) * 128] = block
        for n0 in range(0, width, 512):
            n1 = min(n0 + 512, width)
            h[ch][:, n0:n1] = jnp.dot(
                pk[ch][...], tp[:, n0:n1], preferred_element_type=F32
            ).astype(BF16)
        for p in range(naux):
            lo = p * bs
            if lo + 128 <= width:
                piece = h[ch][:, lo : lo + 128]
            else:
                piece = jnp.concatenate(
                    [h[ch][:, lo:width], jnp.zeros((w, lo + 128 - width), BF16)], axis=1
                )
            hs[ch][p // 4, (p % 4) * w : (p % 4 + 1) * w, :] = piece
        for r in near:
            a2a_copy(ch, *r, False).start()
        a2a_local(ch).start()

    row = lax.broadcasted_iota(jnp.int32, (192, occ), 0)
    col = lax.broadcasted_iota(jnp.int32, (192, occ), 1)
    orbital = (row % 96 // 24 * NC + row // 96) * 20 + row % 24
    spread = jnp.logical_and(orbital == col, row % 24 < 20).astype(BF16)
    for y_ in range(NY):
        for l_ in range(2):
            m = y_ * 2 + l_
            c_, x_, dy_ = place((zh * 2 + l_) * NY + y_)
            ctp[:, m * 128 : (m + 1) * 128] = jnp.dot(
                spread,
                jnp.concatenate([part[c_, x_, dy_] for part in ct], axis=0),
                preferred_element_type=F32,
            ).astype(BF16)

    def rs_copy(ch, d):
        k = (zh + d) % 4
        return pltpu.make_async_remote_copy(
            src_ref=prb[ch].at[pl.ds(pl.multiple_of(k * 48, 16), 48), :], dst_ref=rsb[ch].at[d - 1],
            send_sem=rss.at[ch, d - 1], recv_sem=rsr.at[ch, d - 1],
            device_id=dev((z + 2 * d) % NZ, y, x, c), device_id_type=MESH,
        )

    def ag_copy(ch, d, k):
        part = pf[ch].at[pl.ds(pl.multiple_of(k * 48, 16), 48), :]
        return pltpu.make_async_remote_copy(
            src_ref=part, dst_ref=part,
            send_sem=ags.at[ch, d - 1], recv_sem=agr.at[ch, d - 1],
            device_id=dev((z + 2 * d) % NZ, y, x, c), device_id_type=MESH,
        )

    for ch in range(len(CHUNKS)):
        a2a_local(ch).wait()
        for r in near:
            a2a_copy(ch, *r, True).wait_recv()
        part = lax.dot_general(
            ctp[...], hr[ch][...], (((1,), (1,)), ((), ())), preferred_element_type=F32
        )
        prf[ch][...] = part
        prb[ch][...] = part.astype(BF16)
        for d in range(1, 4):
            rs_copy(ch, d).start()

    mine = pl.ds(pl.multiple_of(zh * 48, 16), 48)
    for ch in range(len(CHUNKS)):
        for d in range(1, 4):
            rs_copy(ch, d).wait_recv()
        whole = prf[ch][mine, :]
        for d in range(1, 4):
            whole = whole + rsb[ch][d - 1].astype(F32)
        pf[ch][mine, :] = (whole * mscale).astype(BF16)
        for d in range(1, 4):
            ag_copy(ch, d, zh).start()

    for ch in range(len(CHUNKS)):
        for d in range(1, 4):
            ag_copy(ch, d, (zh + 4 - d) % 4).wait_recv()
        part = jnp.dot(pf[ch][...], hr[ch][...], preferred_element_type=F32)
        if ch == 0:
            oacc[...] = part
        else:
            oacc[...] += part

    f1 = pltpu.make_async_remote_copy(
        src_ref=oacc.at[pl.ds(pl.multiple_of((1 - c) * 96, 8), 96), :], dst_ref=frecv,
        send_sem=f1s, recv_sem=f1r, device_id=sibling, device_id_type=MESH,
    )
    f1.start()
    f1.wait_recv()
    fsum[...] = oacc[pl.ds(pl.multiple_of(c * 96, 8), 96), :] + frecv[...]

    def f2_copy(i):
        dx, dy, dl = rel[i]
        x_, y_, l_ = (x + dx) % NX, (y + dy) % NY, (zl + dl) % 2
        return pltpu.make_async_remote_copy(
            src_ref=fsum.at[
                pl.ds(pl.multiple_of(x_ * 24, 8), 24),
                pl.ds(pl.multiple_of((y_ * 2 + l_) * 128, 128), 128),
            ],
            dst_ref=f2.at[i], send_sem=f2s.at[i], recv_sem=f2r.at[i],
            device_id=rel_dev(dx, dy, dl), device_id_type=MESH,
        )

    for i in range(len(rel)):
        f2_copy(i).start()
    done = fsum[
        pl.ds(pl.multiple_of(x * 24, 8), 24), pl.ds(pl.multiple_of(m_me * 128, 128), 128)
    ]
    for i in range(len(rel)):
        f2_copy(i).wait_recv()
        done = done + f2[i]
    o_ref[...] = (done * oscale)[:20, :bs]

    for ch in range(len(CHUNKS)):
        for dy in range(1, NY):
            s1_copy(ch, dy).wait_send()
        pl.when(jnp.logical_not(self_here))(lambda ch=ch: s1_copy(ch, 0).wait_send())
        for d in range(1, NX):
            s2_copy(ch, d, x).wait_send()
        core_copy(ch, c).wait_send()
        for r in near:
            a2a_copy(ch, *r, False).wait_send()
        for d in range(1, 4):
            rs_copy(ch, d).wait_send()
            ag_copy(ch, d, zh).wait_send()
    f1.wait_send()
    for i in range(len(rel)):
        f2_copy(i).wait_send()


def shards(three_centre, coeffs, neighbours, counts):
    _, nlist, bs, width = three_centre.shape
    occ = coeffs.shape[1]
    n = len(CHUNKS)
    ws = [w for _, w in CHUNKS]
    dma = pltpu.SemaphoreType.DMA
    scratch = [
        pltpu.VMEM((nlist, bs, width), BF16),
        pltpu.VMEM((nlist * 128, width), BF16),
        pltpu.VMEM((occ, 128), BF16),
        [pltpu.VMEM((NC, NX, NY, w, 128), BF16) for w in ws],
        pltpu.VMEM((192, 1024), BF16),
        [pltpu.VMEM((w, nlist * 128), BF16) for w in ws],
        [pltpu.VMEM((w, width), BF16) for w in ws],
        [pltpu.VMEM((8, 4 * w, 128), BF16) for w in ws],
        [pltpu.VMEM((4 * w, 1024), BF16) for w in ws],
        [pltpu.VMEM((192, 4 * w), F32) for w in ws],
        [pltpu.VMEM((192, 4 * w), BF16) for w in ws],
        [pltpu.VMEM((3, 48, 4 * w), BF16) for w in ws],
        [pltpu.VMEM((192, 4 * w), BF16) for w in ws],
        pltpu.VMEM((192, 1024), F32),
        pltpu.VMEM((96, 1024), F32),
        pltpu.VMEM((96, 1024), F32),
        pltpu.VMEM((31, 24, 128), F32),
        dma((nlist,)),
        dma((n, NY)), dma((n, NY)),
        dma((n, 3)), dma((n, 3)),
        dma((n,)), dma((n,)),
        dma((n, 8)), dma((n, 8)),
        dma((n, 3)), dma((n, 3)),
        dma((n, 3)), dma((n, 3)),
        dma, dma,
        dma((31,)), dma((31,)),
    ]
    return pl.pallas_call(
        kernel,
        out_shape=jax.ShapeDtypeStruct((occ // (NX * NC), bs), F32),
        in_specs=[
            pl.BlockSpec(memory_space=pl.ANY),
            pl.BlockSpec(memory_space=pltpu.VMEM),
            pl.BlockSpec(memory_space=pltpu.SMEM),
            pl.BlockSpec(memory_space=pltpu.SMEM),
        ],
        out_specs=pl.BlockSpec(memory_space=pltpu.VMEM),
        scratch_shapes=scratch,
        compiler_params=pltpu.CompilerParams(
            collective_id=0, has_side_effects=True, vmem_limit_bytes=48 * 2**20
        ),
    )(three_centre, coeffs.T, neighbours, counts).T


def solution(mesh):
    return jax.shard_map(
        shards,
        mesh=mesh,
        in_specs=(P("blk", None, None, "rep"), P("blk", None), P("blk", None), P("blk")),
        out_specs=P("blk", "rep"),
        check_vma=False,
    )
```

```python
import functools
import math

import jax
import jax.numpy as jnp
from jax import lax
from jax.experimental import pallas as pl
from jax.experimental.pallas import tpu as pltpu
from jax.sharding import PartitionSpec as P

MESH = pl.DeviceIdType.MESH
NZ, NY, NX, NC = 8, 4, 4, 2
CHUNKS = ((0, 32), (32, 64), (96, 64))
BF16, F32 = jnp.bfloat16, jnp.float32


def kernel(
    t_ref, c_hbm, nbr_hbm, cnt_hbm, o_ref,
    c_ref, nbr_ref, cnt_ref, tv, tp, own, ct, ctp, pk, h, hs, hr, prf, prb, rsb, pf, oacc, frecv, fsum, fb, f2,
    t_sem, in_sem, s1s, s1r, s2s, s2r, cs, cr, a2s, a2r, rss, rsr, ags, agr, f1s, f1r, f2s, f2r,
):
    occ, bs = c_ref.shape
    nlist = t_ref.shape[1]
    width = t_ref.shape[3]
    naux = width // bs
    total = bs * NZ * NY
    mscale = 1.0 / math.sqrt(total)
    oscale = 1.0 / math.sqrt(naux * NX * NC * occ)
    blk, rep = lax.axis_index("blk"), lax.axis_index("rep")
    z, y, x, c = blk // NY, blk % NY, rep // NC, rep % NC
    zh, zl = z // 2, z % 2
    m_me = y * 2 + zl

    def dev(z_, y_, x_, c_):
        return (z_ * NY + y_, x_ * NC + c_)

    small = [
        pltpu.make_async_copy(src, dst, in_sem.at[i])
        for i, (src, dst) in enumerate(((c_hbm, c_ref), (nbr_hbm, nbr_ref), (cnt_hbm, cnt_ref)))
    ]
    for load in small:
        load.start()
    loads = [pltpu.make_async_copy(t_ref.at[0, l], tv.at[l], t_sem.at[l]) for l in range(nlist)]
    for load in loads:
        load.start()

    sent = []

    def send(copy, when=None):
        def start():
            copy().start()

        def wait():
            copy().wait_send()

        if when is None:
            start()
            sent.append(wait)
        else:
            pl.when(when)(start)
            sent.append(lambda: pl.when(when)(wait))

    def finish():
        while sent:
            sent.pop(0)()

    rel = [(dx, dy, dl) for dx in range(NX) for dy in range(NY) for dl in range(2)][1:]
    rel.sort(key=lambda r: min(r[0], NX - r[0]) + min(r[1], NY - r[1]) + r[2])
    cls = x * NC + c
    self_here = cls == 0

    def s1_shift(dy):
        return lax.rem(cls + 2 * dy, NZ)

    def rel_dev(dx, dy, dl):
        return dev(zh * 2 + (zl + dl) % 2, (y + dy) % NY, (x + dx) % NX, c)

    sibling = dev(z, y, x, 1 - c)
    barrier = pltpu.get_barrier_semaphore()

    def hello(device):
        pl.semaphore_signal(barrier, inc=1, device_id=device, device_id_type=MESH)

    for r in rel:
        hello(rel_dev(*r))
    hello(sibling)
    for d in range(1, NZ // 2):
        hello(dev((z + 2 * d) % NZ, y, x, c))
    for dy in range(NY):
        source = dev((z + NZ - s1_shift(dy)) % NZ, (y + NY - dy) % NY, x, c)
        if dy == 0:
            pl.when(jnp.logical_not(self_here))(functools.partial(hello, source))
        else:
            hello(source)

    for load in small:
        load.wait()
    own[...] = jnp.concatenate([c_ref[...], jnp.zeros((occ, 128 - bs), BF16)], axis=1)

    count = len(rel) + 1 + (NZ // 2 - 1) + NY
    pl.semaphore_wait(barrier, jnp.where(self_here, count - 1, count))

    def s1_copy(ch, dy):
        r0, w = CHUNKS[ch]
        return pltpu.make_async_remote_copy(
            src_ref=own.at[pl.ds(r0, w), :], dst_ref=ct[ch].at[c, x, dy],
            send_sem=s1s.at[ch, dy], recv_sem=s1r.at[ch, dy],
            device_id=dev((z + s1_shift(dy)) % NZ, (y + dy) % NY, x, c), device_id_type=MESH,
        )

    def s1_local(ch):
        r0, w = CHUNKS[ch]
        return pltpu.make_async_copy(own.at[pl.ds(r0, w), :], ct[ch].at[c, x, 0], s1r.at[ch, 0])

    for ch in range(len(CHUNKS)):
        for dy in (2, 1, 3):
            send(functools.partial(s1_copy, ch, dy))
        send(functools.partial(s1_copy, ch, 0), jnp.logical_not(self_here))
        pl.when(self_here)(lambda ch=ch: s1_local(ch).start())

    def s1_wait(ch):
        for dy in range(1, NY):
            s1_copy(ch, dy).wait_recv()
        pl.when(jnp.logical_not(self_here))(lambda: s1_copy(ch, 0).wait_recv())
        pl.when(self_here)(lambda: s1_local(ch).wait())

    def s2_copy(ch, d, x_src):
        part = ct[ch].at[c, x_src]
        return pltpu.make_async_remote_copy(
            src_ref=part, dst_ref=part, send_sem=s2s.at[ch, d - 1], recv_sem=s2r.at[ch, d - 1],
            device_id=dev(z, y, (x + d) % NX, c), device_id_type=MESH,
        )

    def core_copy(ch, c_src):
        part = ct[ch].at[c_src]
        return pltpu.make_async_remote_copy(
            src_ref=part, dst_ref=part, send_sem=cs.at[ch], recv_sem=cr.at[ch],
            device_id=sibling, device_id_type=MESH,
        )

    for l in range(nlist):
        loads[l].wait()
        top = bs // 16 * 16
        tp[l * 128 : l * 128 + top, :] = tv[l, 0:top, :]
        tail = tv[l, top:bs, :]
        tp[l * 128 + top : (l + 1) * 128, :] = jnp.concatenate(
            [tail, jnp.zeros((128 - bs, width), BF16)], axis=0
        )

    for ch in range(len(CHUNKS)):
        s1_wait(ch)
        for d in (2, 1, 3):
            send(functools.partial(s2_copy, ch, d, x))

    def place(b):
        zb, yb = b // NY, b % NY
        dy = (y + NY - yb) % NY
        s = (z + 2 * NZ - zb - 2 * dy) % NZ
        return s % NC, s // NC, dy

    def a2a_copy(ch, to, source):
        lanes = pl.ds(pl.multiple_of(source * 128, 128), 128)
        return pltpu.make_async_remote_copy(
            src_ref=hs[ch].at[to], dst_ref=hr[ch].at[:, lanes],
            send_sem=a2s.at[ch, to], recv_sem=a2r.at[ch, source],
            device_id=dev(zh * 2 + to % 2, to // 2, x, c), device_id_type=MESH,
        )

    def a2a_local(ch, m):
        lanes = pl.ds(m * 128, 128)
        return pltpu.make_async_copy(hs[ch].at[m], hr[ch].at[:, lanes], a2r.at[ch, m])

    for ch, (r0, w) in enumerate(CHUNKS):
        for d in range(1, NX):
            s2_copy(ch, d, (x + NX - d) % NX).wait_recv()
        send(functools.partial(core_copy, ch, c))
        core_copy(ch, 1 - c).wait_recv()
        for l in range(nlist):
            if l == 0:
                block = own[r0 : r0 + w, :]
            else:
                c_, x_, dy_ = place(nbr_ref[0, l])
                block = ct[ch][c_, x_, dy_]
            block = jnp.where(l < cnt_ref[0], block, jnp.zeros_like(block))
            pk[ch][:, l * 128 : (l + 1) * 128] = block
        for m in range(8):
            n0, n1 = m * 512, min((m + 1) * 512, width)
            h[ch][:, n0:n1] = jnp.dot(
                pk[ch][...], tp[:, n0:n1], preferred_element_type=F32
            ).astype(BF16)
            for k in range(4):
                lo = (m * 4 + k) * bs
                if lo + 128 <= width:
                    piece = h[ch][:, lo : lo + 128]
                else:
                    piece = jnp.concatenate(
                        [h[ch][:, lo:width], jnp.zeros((w, lo + 128 - width), BF16)], axis=1
                    )
                hs[ch][m, k * w : (k + 1) * w, :] = piece
            send(functools.partial(a2a_copy, ch, m, m_me), m != m_me)
            pl.when(m == m_me)(lambda m=m: a2a_local(ch, m).start())

    row = lax.broadcasted_iota(jnp.int32, (192, occ), 0)
    col = lax.broadcasted_iota(jnp.int32, (192, occ), 1)
    orbital = (row % 96 // 24 * NC + row // 96) * 20 + row % 24
    spread = jnp.logical_and(orbital == col, row % 24 < 20).astype(BF16)
    for y_ in range(NY):
        for l_ in range(2):
            m = y_ * 2 + l_
            c_, x_, dy_ = place((zh * 2 + l_) * NY + y_)
            ctp[:, m * 128 : (m + 1) * 128] = jnp.dot(
                spread,
                jnp.concatenate([part[c_, x_, dy_] for part in ct], axis=0),
                preferred_element_type=F32,
            ).astype(BF16)

    def rs_copy(ch, d):
        k = (zh + d) % 4
        return pltpu.make_async_remote_copy(
            src_ref=prb[ch].at[pl.ds(pl.multiple_of(k * 48, 16), 48), :], dst_ref=rsb[ch].at[d - 1],
            send_sem=rss.at[ch, d - 1], recv_sem=rsr.at[ch, d - 1],
            device_id=dev((z + 2 * d) % NZ, y, x, c), device_id_type=MESH,
        )

    def ag_copy(ch, d, k):
        part = pf[ch].at[pl.ds(pl.multiple_of(k * 48, 16), 48), :]
        return pltpu.make_async_remote_copy(
            src_ref=part, dst_ref=part,
            send_sem=ags.at[ch, d - 1], recv_sem=agr.at[ch, d - 1],
            device_id=dev((z + 2 * d) % NZ, y, x, c), device_id_type=MESH,
        )

    for ch in range(len(CHUNKS)):
        for m in range(8):
            pl.when(m != m_me)(lambda m=m: a2a_copy(ch, m, m).wait_recv())
            pl.when(m == m_me)(lambda m=m: a2a_local(ch, m).wait())
        part = lax.dot_general(
            ctp[...], hr[ch][...], (((1,), (1,)), ((), ())), preferred_element_type=F32
        )
        prf[ch][...] = part
        prb[ch][...] = part.astype(BF16)
        for d in range(1, 4):
            send(functools.partial(rs_copy, ch, d))

    finish()
    mine = pl.ds(pl.multiple_of(zh * 48, 16), 48)
    for ch in range(len(CHUNKS)):
        for d in range(1, 4):
            rs_copy(ch, d).wait_recv()
        whole = prf[ch][mine, :]
        for d in range(1, 4):
            whole = whole + rsb[ch][d - 1].astype(F32)
        pf[ch][mine, :] = (whole * mscale).astype(BF16)
        for d in range(1, 4):
            send(functools.partial(ag_copy, ch, d, zh))

    for ch in range(len(CHUNKS)):
        for d in range(1, 4):
            ag_copy(ch, d, (zh + 4 - d) % 4).wait_recv()
        part = jnp.dot(pf[ch][...], hr[ch][...], preferred_element_type=F32)
        if ch == 0:
            oacc[...] = part
        else:
            oacc[...] += part

    f1 = pltpu.make_async_remote_copy(
        src_ref=oacc.at[pl.ds(pl.multiple_of((1 - c) * 96, 8), 96), :], dst_ref=frecv,
        send_sem=f1s, recv_sem=f1r, device_id=sibling, device_id_type=MESH,
    )
    send(lambda: f1)
    f1.wait_recv()
    fsum[...] = oacc[pl.ds(pl.multiple_of(c * 96, 8), 96), :] + frecv[...]

    for x_ in range(NX):
        rows = [fsum[x_ * 24 : (x_ + 1) * 24, :], jnp.zeros((8, 1024), F32)]
        fb[x_] = jnp.concatenate(rows, axis=0).astype(BF16)

    def f2_copy(i):
        dx, dy, dl = rel[i]
        x_, y_, l_ = (x + dx) % NX, (y + dy) % NY, (zl + dl) % 2
        return pltpu.make_async_remote_copy(
            src_ref=fb.at[x_, :, pl.ds(pl.multiple_of((y_ * 2 + l_) * 128, 128), 128)],
            dst_ref=f2.at[i], send_sem=f2s.at[i], recv_sem=f2r.at[i],
            device_id=rel_dev(dx, dy, dl), device_id_type=MESH,
        )

    for i in reversed(range(len(rel))):
        send(functools.partial(f2_copy, i))
    finish()
    done = fsum[
        pl.ds(pl.multiple_of(x * 24, 8), 24), pl.ds(pl.multiple_of(m_me * 128, 128), 128)
    ]
    for i in range(len(rel)):
        f2_copy(i).wait_recv()
        done = done + f2[i].astype(F32)[:24]
    o_ref[...] = (done * oscale)[:20, :bs]


def shards(three_centre, coeffs, neighbours, counts):
    _, nlist, bs, width = three_centre.shape
    occ = coeffs.shape[1]
    n = len(CHUNKS)
    ws = [w for _, w in CHUNKS]
    dma = pltpu.SemaphoreType.DMA
    scratch = [
        pltpu.VMEM((occ, bs), BF16),
        pltpu.SMEM((1, nlist), jnp.int32),
        pltpu.SMEM((1,), jnp.int32),
        pltpu.VMEM((nlist, bs, width), BF16),
        pltpu.VMEM((nlist * 128, width), BF16),
        pltpu.VMEM((occ, 128), BF16),
        [pltpu.VMEM((NC, NX, NY, w, 128), BF16) for w in ws],
        pltpu.VMEM((192, 1024), BF16),
        [pltpu.VMEM((w, nlist * 128), BF16) for w in ws],
        [pltpu.VMEM((w, width), BF16) for w in ws],
        [pltpu.VMEM((8, 4 * w, 128), BF16) for w in ws],
        [pltpu.VMEM((4 * w, 1024), BF16) for w in ws],
        [pltpu.VMEM((192, 4 * w), F32) for w in ws],
        [pltpu.VMEM((192, 4 * w), BF16) for w in ws],
        [pltpu.VMEM((3, 48, 4 * w), BF16) for w in ws],
        [pltpu.VMEM((192, 4 * w), BF16) for w in ws],
        pltpu.VMEM((192, 1024), F32),
        pltpu.VMEM((96, 1024), F32),
        pltpu.VMEM((96, 1024), F32),
        pltpu.VMEM((NX, 32, 1024), BF16),
        pltpu.VMEM((31, 32, 128), BF16),
        dma((nlist,)),
        dma((3,)),
        dma((n, NY)), dma((n, NY)),
        dma((n, 3)), dma((n, 3)),
        dma((n,)), dma((n,)),
        dma((n, 8)), dma((n, 8)),
        dma((n, 3)), dma((n, 3)),
        dma((n, 3)), dma((n, 3)),
        dma, dma,
        dma((31,)), dma((31,)),
    ]
    return pl.pallas_call(
        kernel,
        out_shape=jax.ShapeDtypeStruct((occ // (NX * NC), bs), F32),
        in_specs=[
            pl.BlockSpec(memory_space=pl.ANY),
            pl.BlockSpec(memory_space=pl.ANY),
            pl.BlockSpec(memory_space=pl.ANY),
            pl.BlockSpec(memory_space=pl.ANY),
        ],
        out_specs=pl.BlockSpec(memory_space=pltpu.VMEM),
        scratch_shapes=scratch,
        compiler_params=pltpu.CompilerParams(
            collective_id=0, has_side_effects=True, vmem_limit_bytes=60 * 2**20
        ),
    )(three_centre, coeffs.T, neighbours, counts).T


def solution(mesh):
    return jax.shard_map(
        shards,
        mesh=mesh,
        in_specs=(P("blk", None, None, "rep"), P("blk", None), P("blk", None), P("blk")),
        out_specs=P("blk", "rep"),
        check_vma=False,
    )
```

```python
import functools
import math

import jax
import jax.numpy as jnp
from jax import lax
from jax.experimental import pallas as pl
from jax.experimental.pallas import tpu as pltpu
from jax.sharding import PartitionSpec as P

MESH = pl.DeviceIdType.MESH
NZ, NY, NX, NC = 8, 4, 4, 2
CHUNKS = ((0, 32), (32, 64), (96, 64))
ORDER = ("h0", "h1", "h2", "c", "a0", "a1", "r0", "a2", "r1", "r2", "f", "g0", "g1", "g2")
EARLY = 5
BF16, F32 = jnp.bfloat16, jnp.float32


def kernel(
    t_ref, c_hbm, nbr_hbm, cnt_hbm, o_ref,
    c_ref, nbr_ref, cnt_ref, tv, tp, own, ct, ctp, pk, h, hs, hr, prf, prb, rsb, pf, oacc, fa, frecv, fb, ff, f2,
    t_sem, in_sem, s1s, s1r, s2s, s2r, cs, cr, a2s, a2r, rss, rsr, ags, agr, f1s, f1r, f2s, f2r,
):
    occ, bs = c_ref.shape
    nlist = t_ref.shape[1]
    width = t_ref.shape[3]
    naux = width // bs
    total = bs * NZ * NY
    mscale = 1.0 / math.sqrt(total)
    oscale = 1.0 / math.sqrt(naux * NX * NC * occ)
    blk, rep = lax.axis_index("blk"), lax.axis_index("rep")
    z, y, x, c = blk // NY, blk % NY, rep // NC, rep % NC

    def dev(z_, y_, x_, c_):
        return (z_ * NY + y_, x_ * NC + c_)

    small = [
        pltpu.make_async_copy(src, dst, in_sem.at[i])
        for i, (src, dst) in enumerate(((c_hbm, c_ref), (nbr_hbm, nbr_ref), (cnt_hbm, cnt_ref)))
    ]
    for load in small:
        load.start()
    loads = [pltpu.make_async_copy(t_ref.at[0, l], tv.at[l], t_sem.at[l]) for l in range(nlist)]
    for load in loads:
        load.start()

    sent = []

    def send(copy, when=None):
        def start():
            copy().start()

        def wait():
            copy().wait_send()

        if when is None:
            start()
            sent.append(wait)
        else:
            pl.when(when)(start)
            sent.append(lambda: pl.when(when)(wait))

    def finish():
        while sent:
            sent.pop(0)()

    rel = [(dx, dy) for dx in range(NX) for dy in range(NY)][1:]
    rel.sort(key=lambda r: min(r[0], NX - r[0]) + min(r[1], NY - r[1]))
    around = (4, 3, 5, 2, 6, 1, 7)
    cls = x * NC + c
    self_here = cls == 0

    def s1_shift(dy):
        return lax.rem(cls + 2 * dy, NZ)

    def rel_dev(dx, dy):
        return dev(z, (y + dy) % NY, (x + dx) % NX, c)

    sibling = dev(z, y, x, 1 - c)
    barrier = pltpu.get_barrier_semaphore()

    def hello(device):
        pl.semaphore_signal(barrier, inc=1, device_id=device, device_id_type=MESH)

    for r in rel:
        hello(rel_dev(*r))
    hello(sibling)
    for d in around:
        hello(dev((z + d) % NZ, y, x, c))
    for dy in range(NY):
        source = dev((z + NZ - s1_shift(dy)) % NZ, (y + NY - dy) % NY, x, c)
        if dy == 0:
            pl.when(jnp.logical_not(self_here))(functools.partial(hello, source))
        else:
            hello(source)

    for load in small:
        load.wait()
    own[...] = jnp.concatenate([c_ref[...], jnp.zeros((occ, 128 - bs), BF16)], axis=1)

    count = len(rel) + 1 + len(around) + NY
    pl.semaphore_wait(barrier, jnp.where(self_here, count - 1, count))

    def s1_copy(ch, dy):
        r0, w = CHUNKS[ch]
        return pltpu.make_async_remote_copy(
            src_ref=own.at[pl.ds(r0, w), :], dst_ref=ct[ch].at[c, x, dy],
            send_sem=s1s.at[ch, dy], recv_sem=s1r.at[ch, dy],
            device_id=dev((z + s1_shift(dy)) % NZ, (y + dy) % NY, x, c), device_id_type=MESH,
        )

    def s1_local(ch):
        r0, w = CHUNKS[ch]
        return pltpu.make_async_copy(own.at[pl.ds(r0, w), :], ct[ch].at[c, x, 0], s1r.at[ch, 0])

    for ch in range(len(CHUNKS)):
        for dy in (2, 1, 3):
            send(functools.partial(s1_copy, ch, dy))
        send(functools.partial(s1_copy, ch, 0), jnp.logical_not(self_here))
        pl.when(self_here)(lambda ch=ch: s1_local(ch).start())

    def s1_wait(ch):
        for dy in range(1, NY):
            s1_copy(ch, dy).wait_recv()
        pl.when(jnp.logical_not(self_here))(lambda: s1_copy(ch, 0).wait_recv())
        pl.when(self_here)(lambda: s1_local(ch).wait())

    def s2_copy(ch, d, x_src):
        part = ct[ch].at[c, x_src]
        return pltpu.make_async_remote_copy(
            src_ref=part, dst_ref=part, send_sem=s2s.at[ch, d - 1], recv_sem=s2r.at[ch, d - 1],
            device_id=dev(z, y, (x + d) % NX, c), device_id_type=MESH,
        )

    def core_copy(ch, c_src):
        part = ct[ch].at[c_src]
        return pltpu.make_async_remote_copy(
            src_ref=part, dst_ref=part, send_sem=cs.at[ch], recv_sem=cr.at[ch],
            device_id=sibling, device_id_type=MESH,
        )

    for l in range(nlist):
        loads[l].wait()
        top = bs // 16 * 16
        tp[l * 128 : l * 128 + top, :] = tv[l, 0:top, :]
        tail = tv[l, top:bs, :]
        tp[l * 128 + top : (l + 1) * 128, :] = jnp.concatenate(
            [tail, jnp.zeros((128 - bs, width), BF16)], axis=0
        )

    for ch in range(len(CHUNKS)):
        s1_wait(ch)
        for d in (2, 1, 3):
            send(functools.partial(s2_copy, ch, d, x))

    def place(b):
        zb, yb = b // NY, b % NY
        dy = (y + NY - yb) % NY
        s = (z + 2 * NZ - zb - 2 * dy) % NZ
        return s % NC, s // NC, dy

    def a2a_copy(ch, to, source):
        lanes = pl.ds(pl.multiple_of(source * 128, 128), 128)
        return pltpu.make_async_remote_copy(
            src_ref=hs[ch].at[to], dst_ref=hr[ch].at[:, lanes],
            send_sem=a2s.at[ch, to], recv_sem=a2r.at[ch, source],
            device_id=dev(z, to, x, c), device_id_type=MESH,
        )

    def a2a_local(ch, m):
        lanes = pl.ds(m * 128, 128)
        return pltpu.make_async_copy(hs[ch].at[m], hr[ch].at[:, lanes], a2r.at[ch, m])

    def to_sibling(ch):
        for d in range(1, NX):
            s2_copy(ch, d, (x + NX - d) % NX).wait_recv()
        send(functools.partial(core_copy, ch, c))

    def halves(ch):
        r0, w = CHUNKS[ch]
        if ch == 0:
            to_sibling(0)
        core_copy(ch, 1 - c).wait_recv()
        for l in range(nlist):
            if l == 0:
                block = own[r0 : r0 + w, :]
            else:
                c_, x_, dy_ = place(nbr_ref[0, l])
                block = ct[ch][c_, x_, dy_]
            block = jnp.where(l < cnt_ref[0], block, jnp.zeros_like(block))
            pk[ch][:, l * 128 : (l + 1) * 128] = block
        for m in range(8):
            n0, n1 = m * 512, min((m + 1) * 512, width)
            h[ch][:, n0:n1] = jnp.dot(
                pk[ch][...], tp[:, n0:n1], preferred_element_type=F32
            ).astype(BF16)
            for k in range(4):
                lo = (m * 4 + k) * bs
                if lo + 128 <= width:
                    piece = h[ch][:, lo : lo + 128]
                else:
                    piece = jnp.concatenate(
                        [h[ch][:, lo:width], jnp.zeros((w, lo + 128 - width), BF16)], axis=1
                    )
                r0 = (m % 2 * 4 + k) * w
                hs[ch][m // 2, r0 : r0 + w, :] = piece
            if m % 2:
                to = m // 2
                send(functools.partial(a2a_copy, ch, to, y), to != y)
                pl.when(to == y)(lambda to=to: a2a_local(ch, to).start())
            if m == EARLY and ch + 1 < len(CHUNKS):
                to_sibling(ch + 1)

    def group():
        row = lax.broadcasted_iota(jnp.int32, (256, occ), 0)
        col = lax.broadcasted_iota(jnp.int32, (256, occ), 1)
        first = (row % 64 // 16 * NC + row // 64) * 20 + row % 16
        last = (row % 16 // 4 * NC + row % 32 // 16) * 20 + 16 + row % 4
        spread = (jnp.where(row < 128, first, last) == col).astype(BF16)
        for y_ in range(NY):
            c_, x_, dy_ = place(z * NY + y_)
            ctp[:, y_ * 128 : (y_ + 1) * 128] = jnp.dot(
                spread,
                jnp.concatenate([part[c_, x_, dy_] for part in ct], axis=0),
                preferred_element_type=F32,
            ).astype(BF16)

    def rs_copy(ch, d):
        return pltpu.make_async_remote_copy(
            src_ref=prb[ch].at[(z + d) % NZ], dst_ref=rsb[ch].at[d - 1],
            send_sem=rss.at[ch, d - 1], recv_sem=rsr.at[ch, d - 1],
            device_id=dev((z + d) % NZ, y, x, c), device_id_type=MESH,
        )

    def ag_copy(ch, d, k):
        part = pf[ch].at[k]
        return pltpu.make_async_remote_copy(
            src_ref=part, dst_ref=part,
            send_sem=ags.at[ch, d - 1], recv_sem=agr.at[ch, d - 1],
            device_id=dev((z + d) % NZ, y, x, c), device_id_type=MESH,
        )

    def pair(ch):
        w = CHUNKS[ch][1]
        q, full = w // 4, padded(w)
        for m in range(NY):
            pl.when(m != y)(lambda m=m: a2a_copy(ch, m, m).wait_recv())
            pl.when(m == y)(lambda m=m: a2a_local(ch, m).wait())
        part = lax.dot_general(
            hr[ch][...], ctp[...], (((1,), (1,)), ((), ())), preferred_element_type=F32
        )
        quarter = lax.broadcasted_iota(jnp.int32, (q, 128), 1) // 32
        for k in range(NZ):
            tail = jnp.zeros((q, 128), F32)
            for i in range(4):
                r0 = k * w + i * q
                tail = jnp.where(quarter == i, part[r0 : r0 + q, 128:], tail)
            rows = [part[k * w : (k + 1) * w, :128], tail]
            if full > w + q:
                rows.append(jnp.zeros((full - w - q, 128), F32))
            rows = jnp.concatenate(rows, axis=0)
            prf[ch][k] = rows
            prb[ch][k] = rows.astype(BF16)
        for d in around:
            send(functools.partial(rs_copy, ch, d))

    def reduce(ch):
        for d in around:
            rs_copy(ch, d).wait_recv()
        whole = prf[ch][z]
        for d in around:
            whole = whole + rsb[ch][d - 1].astype(F32)
        pf[ch][z] = (whole * mscale).astype(BF16)
        for d in around:
            send(functools.partial(ag_copy, ch, d, z))

    def apply(ch):
        w = CHUNKS[ch][1]
        q = w // 4
        for d in around:
            ag_copy(ch, d, (z + NZ - d) % NZ).wait_recv()
        quarter = lax.broadcasted_iota(jnp.int32, (q, 128), 1) // 32
        firsts, lasts = [], []
        for k in range(NZ):
            firsts.append(pf[ch][k, 0:w, :])
            tail = pf[ch][k].astype(F32)[w : w + q]
            for i in range(4):
                lasts.append(jnp.where(quarter == i, tail, 0.0))
        left = jnp.concatenate(
            [jnp.concatenate(firsts, axis=0), jnp.concatenate(lasts, axis=0).astype(BF16)], axis=1
        )
        part = lax.dot_general(
            left, hr[ch][...], (((0,), (0,)), ((), ())), preferred_element_type=F32
        )
        if ch == 0:
            oacc[...] = part
        else:
            oacc[...] += part

    steps = {"h": halves, "a": pair, "r": reduce, "g": apply}
    for step in ORDER:
        if step == "c":
            group()
        elif step == "f":
            finish()
        else:
            steps[step[0]](int(step[1:]))

    lasts = oacc[128:160, :] + oacc[160:192, :] + oacc[192:224, :] + oacc[224:256, :]
    for c_ in range(NC):
        fa[c_, 0:64, :] = oacc[c_ * 64 : (c_ + 1) * 64, :]
        fa[c_, 64:80, :] = lasts[c_ * 16 : (c_ + 1) * 16]
    f1 = pltpu.make_async_remote_copy(
        src_ref=fa.at[1 - c], dst_ref=frecv,
        send_sem=f1s, recv_sem=f1r, device_id=sibling, device_id_type=MESH,
    )
    send(lambda: f1)
    f1.wait_recv()
    fsum = fa[c] + frecv[...]
    for x_ in range(NX):
        rows = [
            fsum[x_ * 16 : (x_ + 1) * 16],
            fsum[64 + x_ * 4 : 64 + (x_ + 1) * 4],
            jnp.zeros((12, NY * 128), F32),
        ]
        rows = jnp.concatenate(rows, axis=0)
        fb[x_] = rows.astype(BF16)
        ff[x_] = rows

    def f2_copy(i):
        dx, dy = rel[i]
        x_, y_ = (x + dx) % NX, (y + dy) % NY
        return pltpu.make_async_remote_copy(
            src_ref=fb.at[x_, :, pl.ds(pl.multiple_of(y_ * 128, 128), 128)],
            dst_ref=f2.at[i], send_sem=f2s.at[i], recv_sem=f2r.at[i],
            device_id=rel_dev(dx, dy), device_id_type=MESH,
        )

    for i in reversed(range(len(rel))):
        send(functools.partial(f2_copy, i))
    finish()
    done = ff[x, :, pl.ds(pl.multiple_of(y * 128, 128), 128)]
    for i in range(len(rel)):
        f2_copy(i).wait_recv()
        done = done + f2[i].astype(F32)
    o_ref[...] = (done * oscale)[:20, :bs]


def padded(w):
    return (w + w // 4 + 15) // 16 * 16


def shards(three_centre, coeffs, neighbours, counts):
    _, nlist, bs, width = three_centre.shape
    occ = coeffs.shape[1]
    n = len(CHUNKS)
    ws = [w for _, w in CHUNKS]
    dma = pltpu.SemaphoreType.DMA
    scratch = [
        pltpu.VMEM((occ, bs), BF16),
        pltpu.SMEM((1, nlist), jnp.int32),
        pltpu.SMEM((1,), jnp.int32),
        pltpu.VMEM((nlist, bs, width), BF16),
        pltpu.VMEM((nlist * 128, width), BF16),
        pltpu.VMEM((occ, 128), BF16),
        [pltpu.VMEM((NC, NX, NY, w, 128), BF16) for w in ws],
        pltpu.VMEM((256, NY * 128), BF16),
        [pltpu.VMEM((w, nlist * 128), BF16) for w in ws],
        [pltpu.VMEM((w, width), BF16) for w in ws],
        [pltpu.VMEM((NY, NZ * w, 128), BF16) for w in ws],
        [pltpu.VMEM((NZ * w, NY * 128), BF16) for w in ws],
        [pltpu.VMEM((NZ, padded(w), 128), F32) for w in ws],
        [pltpu.VMEM((NZ, padded(w), 128), BF16) for w in ws],
        [pltpu.VMEM((NZ - 1, padded(w), 128), BF16) for w in ws],
        [pltpu.VMEM((NZ, padded(w), 128), BF16) for w in ws],
        pltpu.VMEM((256, NY * 128), F32),
        pltpu.VMEM((NC, 80, NY * 128), F32),
        pltpu.VMEM((80, NY * 128), F32),
        pltpu.VMEM((NX, 32, NY * 128), BF16),
        pltpu.VMEM((NX, 32, NY * 128), F32),
        pltpu.VMEM((15, 32, 128), BF16),
        dma((nlist,)),
        dma((3,)),
        dma((n, NY)), dma((n, NY)),
        dma((n, 3)), dma((n, 3)),
        dma((n,)), dma((n,)),
        dma((n, NY)), dma((n, NY)),
        dma((n, NZ - 1)), dma((n, NZ - 1)),
        dma((n, NZ - 1)), dma((n, NZ - 1)),
        dma, dma,
        dma((15,)), dma((15,)),
    ]
    return pl.pallas_call(
        kernel,
        out_shape=jax.ShapeDtypeStruct((occ // (NX * NC), bs), F32),
        in_specs=[
            pl.BlockSpec(memory_space=pl.ANY),
            pl.BlockSpec(memory_space=pl.ANY),
            pl.BlockSpec(memory_space=pl.ANY),
            pl.BlockSpec(memory_space=pl.ANY),
        ],
        out_specs=pl.BlockSpec(memory_space=pltpu.VMEM),
        scratch_shapes=scratch,
        compiler_params=pltpu.CompilerParams(
            collective_id=0, has_side_effects=True, vmem_limit_bytes=60 * 2**20
        ),
    )(three_centre, coeffs.T, neighbours, counts).T


def solution(mesh):
    return jax.shard_map(
        shards,
        mesh=mesh,
        in_specs=(P("blk", None, None, "rep"), P("blk", None), P("blk", None), P("blk")),
        out_specs=P("blk", "rep"),
        check_vma=False,
    )
```

```python
import functools
import math

import jax
import jax.numpy as jnp
from jax import lax
from jax.experimental import pallas as pl
from jax.experimental.pallas import tpu as pltpu
from jax.sharding import PartitionSpec as P

MESH = pl.DeviceIdType.MESH
NZ, NY, NX, NC = 8, 4, 4, 2
CHUNKS = ((0, 32), (32, 64), (96, 64))
ORDER = ("h0", "h1", "h2", "c", "a0", "a1", "r0", "a2", "r1", "r2", "f", "g0", "g1", "g2")
EARLY = 5
BF16, F32 = jnp.bfloat16, jnp.float32


def kernel(
    t_ref, c_hbm, nbr_hbm, cnt_hbm, o_ref,
    c_ref, nbr_ref, cnt_ref, tv, tp, own, ct, ctp, pk, h, hs, hr, prf, prb, rsb, pf, oacc, fa, frecv, fb, ff, f2,
    t_sem, in_sem, s1s, s1r, s2s, s2r, cs, cr, a2s, a2r, rss, rsr, ags, agr, f1s, f1r, f2s, f2r,
):
    occ, bs = c_ref.shape
    nlist = t_ref.shape[1]
    width = t_ref.shape[3]
    naux = width // bs
    total = bs * NZ * NY
    mscale = 1.0 / math.sqrt(total)
    oscale = 1.0 / math.sqrt(naux * NX * NC * occ)
    blk, rep = lax.axis_index("blk"), lax.axis_index("rep")
    z, y, x, c = blk // NY, blk % NY, rep // NC, rep % NC

    def dev(z_, y_, x_, c_):
        return (z_ * NY + y_, x_ * NC + c_)

    small = [
        pltpu.make_async_copy(src, dst, in_sem.at[i])
        for i, (src, dst) in enumerate(((c_hbm, c_ref), (nbr_hbm, nbr_ref), (cnt_hbm, cnt_ref)))
    ]
    for load in small:
        load.start()
    loads = [pltpu.make_async_copy(t_ref.at[0, l], tv.at[l], t_sem.at[l]) for l in range(nlist)]
    for load in loads:
        load.start()

    sent = []

    def send(copy, when=None):
        def start():
            copy().start()

        def wait():
            copy().wait_send()

        if when is None:
            start()
            sent.append(wait)
        else:
            pl.when(when)(start)
            sent.append(lambda: pl.when(when)(wait))

    def finish():
        while sent:
            sent.pop(0)()

    rel = [(dx, dy) for dx in range(NX) for dy in range(NY)][1:]
    rel.sort(key=lambda r: min(r[0], NX - r[0]) + min(r[1], NY - r[1]))
    around = (4, 3, 5, 2, 6, 1, 7)
    cls = x * NC + c
    self_here = cls == 0

    def rel_dev(dx, dy):
        return dev(z, (y + dy) % NY, (x + dx) % NX, c)

    sibling = dev(z, y, x, 1 - c)
    barrier = pltpu.get_barrier_semaphore()

    def hello(device):
        pl.semaphore_signal(barrier, inc=1, device_id=device, device_id_type=MESH)

    for r in rel:
        hello(rel_dev(*r))
    hello(sibling)
    for d in around:
        hello(dev((z + d) % NZ, y, x, c))

    for load in small:
        load.wait()
    own[...] = jnp.concatenate([c_ref[...], jnp.zeros((occ, 128 - bs), BF16)], axis=1)

    pl.semaphore_wait(barrier, len(rel) + 1 + len(around))

    def s1_copy(ch):
        r0, w = CHUNKS[ch]
        return pltpu.make_async_remote_copy(
            src_ref=own.at[pl.ds(r0, w), :], dst_ref=ct[ch].at[c, x, 0],
            send_sem=s1s.at[ch], recv_sem=s1r.at[ch],
            device_id=dev((z + cls) % NZ, y, x, c), device_id_type=MESH,
        )

    def s1_local(ch):
        r0, w = CHUNKS[ch]
        return pltpu.make_async_copy(own.at[pl.ds(r0, w), :], ct[ch].at[c, x, 0], s1r.at[ch])

    for ch in range(len(CHUNKS)):
        send(functools.partial(s1_copy, ch), jnp.logical_not(self_here))
        pl.when(self_here)(lambda ch=ch: s1_local(ch).start())

    def s1_wait(ch):
        pl.when(jnp.logical_not(self_here))(lambda: s1_copy(ch).wait_recv())
        pl.when(self_here)(lambda: s1_local(ch).wait())

    def s2_copy(ch, i, x_src):
        dx, dy = rel[i]
        return pltpu.make_async_remote_copy(
            src_ref=ct[ch].at[c, x, 0], dst_ref=ct[ch].at[c, x_src, dy],
            send_sem=s2s.at[ch, i], recv_sem=s2r.at[ch, i],
            device_id=rel_dev(dx, dy), device_id_type=MESH,
        )

    def core_copy(ch, c_src):
        part = ct[ch].at[c_src]
        return pltpu.make_async_remote_copy(
            src_ref=part, dst_ref=part, send_sem=cs.at[ch], recv_sem=cr.at[ch],
            device_id=sibling, device_id_type=MESH,
        )

    for l in range(nlist):
        loads[l].wait()
        top = bs // 16 * 16
        tp[l * 128 : l * 128 + top, :] = tv[l, 0:top, :]
        tail = tv[l, top:bs, :]
        tp[l * 128 + top : (l + 1) * 128, :] = jnp.concatenate(
            [tail, jnp.zeros((128 - bs, width), BF16)], axis=0
        )

    for ch in range(len(CHUNKS)):
        s1_wait(ch)
        for i in reversed(range(len(rel))):
            send(functools.partial(s2_copy, ch, i, x))

    def place(b):
        zb, yb = b // NY, b % NY
        s = (z + NZ - zb) % NZ
        return s % NC, s // NC, (y + NY - yb) % NY

    def a2a_copy(ch, to, source):
        lanes = pl.ds(pl.multiple_of(source * 128, 128), 128)
        return pltpu.make_async_remote_copy(
            src_ref=hs[ch].at[to], dst_ref=hr[ch].at[:, lanes],
            send_sem=a2s.at[ch, to], recv_sem=a2r.at[ch, source],
            device_id=dev(z, to, x, c), device_id_type=MESH,
        )

    def a2a_local(ch, m):
        lanes = pl.ds(m * 128, 128)
        return pltpu.make_async_copy(hs[ch].at[m], hr[ch].at[:, lanes], a2r.at[ch, m])

    def to_sibling(ch):
        for i in range(len(rel)):
            s2_copy(ch, i, (x + NX - rel[i][0]) % NX).wait_recv()
        send(functools.partial(core_copy, ch, c))

    def halves(ch):
        r0, w = CHUNKS[ch]
        if ch == 0:
            to_sibling(0)
        core_copy(ch, 1 - c).wait_recv()
        for l in range(nlist):
            if l == 0:
                block = own[r0 : r0 + w, :]
            else:
                c_, x_, dy_ = place(nbr_ref[0, l])
                block = ct[ch][c_, x_, dy_]
            block = jnp.where(l < cnt_ref[0], block, jnp.zeros_like(block))
            pk[ch][:, l * 128 : (l + 1) * 128] = block
        for m in range(8):
            n0, n1 = m * 512, min((m + 1) * 512, width)
            h[ch][:, n0:n1] = jnp.dot(
                pk[ch][...], tp[:, n0:n1], preferred_element_type=F32
            ).astype(BF16)
            for k in range(4):
                lo = (m * 4 + k) * bs
                if lo + 128 <= width:
                    piece = h[ch][:, lo : lo + 128]
                else:
                    piece = jnp.concatenate(
                        [h[ch][:, lo:width], jnp.zeros((w, lo + 128 - width), BF16)], axis=1
                    )
                r0 = (m % 2 * 4 + k) * w
                hs[ch][m // 2, r0 : r0 + w, :] = piece
            if m % 2:
                to = m // 2
                send(functools.partial(a2a_copy, ch, to, y), to != y)
                pl.when(to == y)(lambda to=to: a2a_local(ch, to).start())
            if m == EARLY and ch + 1 < len(CHUNKS):
                to_sibling(ch + 1)

    def group():
        row = lax.broadcasted_iota(jnp.int32, (256, occ), 0)
        col = lax.broadcasted_iota(jnp.int32, (256, occ), 1)
        first = (row % 64 // 16 * NC + row // 64) * 20 + row % 16
        last = (row % 16 // 4 * NC + row % 32 // 16) * 20 + 16 + row % 4
        spread = (jnp.where(row < 128, first, last) == col).astype(BF16)
        for y_ in range(NY):
            c_, x_, dy_ = place(z * NY + y_)
            ctp[:, y_ * 128 : (y_ + 1) * 128] = jnp.dot(
                spread,
                jnp.concatenate([part[c_, x_, dy_] for part in ct], axis=0),
                preferred_element_type=F32,
            ).astype(BF16)

    def rs_copy(ch, d):
        return pltpu.make_async_remote_copy(
            src_ref=prb[ch].at[(z + d) % NZ], dst_ref=rsb[ch].at[d - 1],
            send_sem=rss.at[ch, d - 1], recv_sem=rsr.at[ch, d - 1],
            device_id=dev((z + d) % NZ, y, x, c), device_id_type=MESH,
        )

    def ag_copy(ch, d, k):
        part = pf[ch].at[k]
        return pltpu.make_async_remote_copy(
            src_ref=part, dst_ref=part,
            send_sem=ags.at[ch, d - 1], recv_sem=agr.at[ch, d - 1],
            device_id=dev((z + d) % NZ, y, x, c), device_id_type=MESH,
        )

    def pair(ch):
        w = CHUNKS[ch][1]
        q, full = w // 4, padded(w)
        for m in range(NY):
            pl.when(m != y)(lambda m=m: a2a_copy(ch, m, m).wait_recv())
            pl.when(m == y)(lambda m=m: a2a_local(ch, m).wait())
        part = lax.dot_general(
            hr[ch][...], ctp[...], (((1,), (1,)), ((), ())), preferred_element_type=F32
        )
        quarter = lax.broadcasted_iota(jnp.int32, (q, 128), 1) // 32
        for k in range(NZ):
            tail = jnp.zeros((q, 128), F32)
            for i in range(4):
                r0 = k * w + i * q
                tail = jnp.where(quarter == i, part[r0 : r0 + q, 128:], tail)
            rows = [part[k * w : (k + 1) * w, :128], tail]
            if full > w + q:
                rows.append(jnp.zeros((full - w - q, 128), F32))
            rows = jnp.concatenate(rows, axis=0)
            prf[ch][k] = rows
            prb[ch][k] = rows.astype(BF16)
        for d in around:
            send(functools.partial(rs_copy, ch, d))

    def reduce(ch):
        for d in around:
            rs_copy(ch, d).wait_recv()
        whole = prf[ch][z]
        for d in around:
            whole = whole + rsb[ch][d - 1].astype(F32)
        pf[ch][z] = (whole * mscale).astype(BF16)
        for d in around:
            send(functools.partial(ag_copy, ch, d, z))

    def apply(ch):
        w = CHUNKS[ch][1]
        q = w // 4
        for d in around:
            ag_copy(ch, d, (z + NZ - d) % NZ).wait_recv()
        quarter = lax.broadcasted_iota(jnp.int32, (q, 128), 1) // 32
        firsts, lasts = [], []
        for k in range(NZ):
            firsts.append(pf[ch][k, 0:w, :])
            tail = pf[ch][k].astype(F32)[w : w + q]
            for i in range(4):
                lasts.append(jnp.where(quarter == i, tail, 0.0))
        left = jnp.concatenate(
            [jnp.concatenate(firsts, axis=0), jnp.concatenate(lasts, axis=0).astype(BF16)], axis=1
        )
        part = lax.dot_general(
            left, hr[ch][...], (((0,), (0,)), ((), ())), preferred_element_type=F32
        )
        if ch == 0:
            oacc[...] = part
        else:
            oacc[...] += part

    steps = {"h": halves, "a": pair, "r": reduce, "g": apply}
    for step in ORDER:
        if step == "c":
            group()
        elif step == "f":
            finish()
        else:
            steps[step[0]](int(step[1:]))

    lasts = oacc[128:160, :] + oacc[160:192, :] + oacc[192:224, :] + oacc[224:256, :]
    for c_ in range(NC):
        fa[c_, 0:64, :] = oacc[c_ * 64 : (c_ + 1) * 64, :]
        fa[c_, 64:80, :] = lasts[c_ * 16 : (c_ + 1) * 16]
    f1 = pltpu.make_async_remote_copy(
        src_ref=fa.at[1 - c], dst_ref=frecv,
        send_sem=f1s, recv_sem=f1r, device_id=sibling, device_id_type=MESH,
    )
    send(lambda: f1)
    f1.wait_recv()
    fsum = fa[c] + frecv[...]
    for x_ in range(NX):
        rows = [
            fsum[x_ * 16 : (x_ + 1) * 16],
            fsum[64 + x_ * 4 : 64 + (x_ + 1) * 4],
            jnp.zeros((12, NY * 128), F32),
        ]
        rows = jnp.concatenate(rows, axis=0)
        fb[x_] = rows.astype(BF16)
        ff[x_] = rows

    def f2_copy(i):
        dx, dy = rel[i]
        x_, y_ = (x + dx) % NX, (y + dy) % NY
        return pltpu.make_async_remote_copy(
            src_ref=fb.at[x_, :, pl.ds(pl.multiple_of(y_ * 128, 128), 128)],
            dst_ref=f2.at[i], send_sem=f2s.at[i], recv_sem=f2r.at[i],
            device_id=rel_dev(dx, dy), device_id_type=MESH,
        )

    for i in reversed(range(len(rel))):
        send(functools.partial(f2_copy, i))
    finish()
    done = ff[x, :, pl.ds(pl.multiple_of(y * 128, 128), 128)]
    for i in range(len(rel)):
        f2_copy(i).wait_recv()
        done = done + f2[i].astype(F32)
    o_ref[...] = (done * oscale)[:20, :bs]


def padded(w):
    return (w + w // 4 + 15) // 16 * 16


def shards(three_centre, coeffs, neighbours, counts):
    _, nlist, bs, width = three_centre.shape
    occ = coeffs.shape[1]
    n = len(CHUNKS)
    ws = [w for _, w in CHUNKS]
    dma = pltpu.SemaphoreType.DMA
    scratch = [
        pltpu.VMEM((occ, bs), BF16),
        pltpu.SMEM((1, nlist), jnp.int32),
        pltpu.SMEM((1,), jnp.int32),
        pltpu.VMEM((nlist, bs, width), BF16),
        pltpu.VMEM((nlist * 128, width), BF16),
        pltpu.VMEM((occ, 128), BF16),
        [pltpu.VMEM((NC, NX, NY, w, 128), BF16) for w in ws],
        pltpu.VMEM((256, NY * 128), BF16),
        [pltpu.VMEM((w, nlist * 128), BF16) for w in ws],
        [pltpu.VMEM((w, width), BF16) for w in ws],
        [pltpu.VMEM((NY, NZ * w, 128), BF16) for w in ws],
        [pltpu.VMEM((NZ * w, NY * 128), BF16) for w in ws],
        [pltpu.VMEM((NZ, padded(w), 128), F32) for w in ws],
        [pltpu.VMEM((NZ, padded(w), 128), BF16) for w in ws],
        [pltpu.VMEM((NZ - 1, padded(w), 128), BF16) for w in ws],
        [pltpu.VMEM((NZ, padded(w), 128), BF16) for w in ws],
        pltpu.VMEM((256, NY * 128), F32),
        pltpu.VMEM((NC, 80, NY * 128), F32),
        pltpu.VMEM((80, NY * 128), F32),
        pltpu.VMEM((NX, 32, NY * 128), BF16),
        pltpu.VMEM((NX, 32, NY * 128), F32),
        pltpu.VMEM((15, 32, 128), BF16),
        dma((nlist,)),
        dma((3,)),
        dma((n,)), dma((n,)),
        dma((n, 15)), dma((n, 15)),
        dma((n,)), dma((n,)),
        dma((n, NY)), dma((n, NY)),
        dma((n, NZ - 1)), dma((n, NZ - 1)),
        dma((n, NZ - 1)), dma((n, NZ - 1)),
        dma, dma,
        dma((15,)), dma((15,)),
    ]
    return pl.pallas_call(
        kernel,
        out_shape=jax.ShapeDtypeStruct((occ // (NX * NC), bs), F32),
        in_specs=[
            pl.BlockSpec(memory_space=pl.ANY),
            pl.BlockSpec(memory_space=pl.ANY),
            pl.BlockSpec(memory_space=pl.ANY),
            pl.BlockSpec(memory_space=pl.ANY),
        ],
        out_specs=pl.BlockSpec(memory_space=pltpu.VMEM),
        scratch_shapes=scratch,
        compiler_params=pltpu.CompilerParams(
            collective_id=0, has_side_effects=True, vmem_limit_bytes=60 * 2**20
        ),
    )(three_centre, coeffs.T, neighbours, counts).T


def solution(mesh):
    return jax.shard_map(
        shards,
        mesh=mesh,
        in_specs=(P("blk", None, None, "rep"), P("blk", None), P("blk", None), P("blk")),
        out_specs=P("blk", "rep"),
        check_vma=False,
    )
```
